32 devices in a mesh: groups: 2 (over y), dp: 4 (over z), seq: 2 (over x), head: 2 (over core).
Axes of the slice: x: 2, y: 2, z: 4, core: 2. Of those that a mesh axis runs over, the one named last changes fastest.
Arguments:
- projected: bfloat16 [3, 2048, 16, 2, 128], P(None, ('groups', 'dp', 'seq'), None, 'head'), parts along dimension 1, may hold values from -60 to 60
- assignment: int32 [8, 2, 4], P(('groups', 'dp'), 'seq'), parts along dimension 0, may hold values from 0 to 3, as said below
- segments: int32 [8, 256], P(('groups', 'dp')), parts along dimension 0, may hold values from 0 to 3, never falling along the last dimension, each value on 1 to 192 neighbouring positions
- advantage: float32 [8, 4], P(('groups', 'dp')), parts along dimension 0, may hold values from -4 to 4
- out_weight: bfloat16 [16, 2, 128, 5120], P('dp', 'head', None, 'seq'), may hold values from -0.09375 to 0.09375
- cotangent: bfloat16 [2048, 5120], P(('groups', 'dp'), 'seq'), parts along dimension 0, may hold values from -6 to 6
Outputs:
- mixed: bfloat16 [2048, 5120], P(('groups', 'dp'), ('seq', 'head')), parts along dimension 0
- weight_grad: float32 [32, 2, 128, 5120], P(('groups', 'dp'), 'head', None, 'seq'), parts along dimension 0
The draws below stay inside these ranges and needn't reach their ends.
There are 2 independent parts, one for each index of `groups`. The reference program is written for one: setup_inputs(seed, part) draws one part's arguments, and reference() takes and returns one part's arrays. A program takes and returns all parts, laid end to end along the dimension named above; an argument that names none is the same for every part. Nothing has to cross between parts.
Inputs may be any that keep to these rules, and one draw needn't show every extreme that they name: `assignment`: for each sequence shard, every trainer row receives exactly 4 blocks and at most 2 from one owner; every owner sends 2 blocks to some trainer row.
All inputs are finite; a program needn't handle non-finite values.
Results may differ from the reference program's by a relative error of at most 0.008.
Values may be sent and summed in bfloat16 or wider, within the bound.
No kernel may reach another device: no remote copies, remote signals or barrier semaphores. Data moves between devices by JAX's collectives and lax.ppermute only.
A program may use at most 128 MiB of HBM per device.

```python
import math
import jax
import jax.numpy as jnp
import numpy as np
from jax import lax

D = 5120
HEADS = 32
HS = 128
HPAIR = 16
SEGS = 4
BLK = 32
NBLK = 4
ROW = 256
TOKENS = 1024
MOST = 192
N_DP = 4
N_SEQ = 2


def draw_projected(key, part):
    key = jax.random.fold_in(key, 11)
    shape = (3, TOKENS, HPAIR, 2, HS)
    full = jnp.clip(jax.random.normal(key, shape, jnp.float32), -6.0, 6.0)
    return full.astype(jnp.bfloat16)


def draw_assignment(key, part):
    key = jax.random.fold_in(key, 23)

    def one_shard(sub):
        keys_four = jax.random.split(sub, 4)
        owners = jax.random.permutation(keys_four[0], N_DP)
        trainers = jax.random.permutation(keys_four[1], N_DP)
        shift_order = jax.random.permutation(keys_four[2], N_DP)
        doubled = N_DP // 4
        index = jnp.arange(N_DP, dtype=jnp.int32)
        shift_pick = shift_order[jnp.where(index < 2 * doubled, index // 2, index - doubled)]
        targets = trainers[(index[:, None] + shift_pick[None, :]) % N_DP]
        targets = targets[owners]
        shuffles = jax.vmap(lambda sub_key: jax.random.permutation(sub_key, N_DP))(jax.random.split(keys_four[3], N_DP))
        return jnp.take_along_axis(targets, shuffles, axis=1)
    every = jax.vmap(one_shard)(jax.random.split(key, N_SEQ))
    return jnp.transpose(every, (1, 0, 2)).astype(jnp.int32)


def shard_levels(key, extent, cuts, least, high):
    factor_of = 1.0
    for position, parts in cuts:
        draws = jax.random.uniform(jax.random.fold_in(jax.random.fold_in(key, 6), position), (parts,), jnp.float32, least / len(cuts), high / len(cuts))
        factor_of = factor_of * jnp.repeat(jnp.exp(draws), extent[position] // parts).reshape((-1,) + (1,) * (len(extent) - 1 - position))
    return factor_of


def length_profile(amount, total, most, slope):
    portions = [(1 << 20) // math.isqrt(standing ** slope) + 1 for standing in range(2, amount + 1)]
    surplus, holding = total - most - (amount - 1), [1] * (amount - 1)
    while surplus > 0:
        candidates = [i for i in range(amount - 1) if holding[i] < most]
        mass, budget = sum([portions[i] for i in candidates]), surplus
        for i in candidates:
            extra = min(most - holding[i], max(1, budget * portions[i] // mass), surplus)
            holding[i] = holding[i] + extra
            surplus = surplus - extra
    return np.array([most] + holding)


def ragged_sizes(own_key, amount, total, bound, skew):
    if amount == 2:
        one = jax.random.randint(own_key, (), max(1, total - bound), min(bound, total - 1) + 1)
        return jnp.stack([one, total - one])
    sizes = jnp.asarray(length_profile(amount, total, bound, skew), jnp.int32)
    pairs = (amount - 1) // 2
    giver, taker = sizes[1:1 + 2 * pairs:2], sizes[2:2 + 2 * pairs:2]
    slack = jnp.minimum(giver - 1, bound - taker)
    passed = jax.random.randint(jax.random.fold_in(own_key, 1), (pairs,), 0, 1 << 20) % (slack + 1)
    sizes = sizes.at[1:1 + 2 * pairs:2].set(giver - passed).at[2:2 + 2 * pairs:2].set(taker + passed)
    return sizes[jax.random.permutation(jax.random.fold_in(own_key, 2), amount)]


def normal_values(key, extent, deviation, reach, cuts=(), kind=jnp.bfloat16):
    entries = jax.random.normal(key, extent, jnp.float32) * deviation
    if len(cuts) > 0:
        entries = shard_levels(key, extent, cuts, -0.22, 0.18) * entries
    return jnp.clip(entries, min=-reach, max=reach).astype(kind)


def setup_inputs(seed: int = 0, part: int = 0) -> dict:
    key_list = jax.random.split(jax.random.key(seed), 7)
    part_keys = jax.random.split(jax.random.fold_in(key_list[6], part), 7)
    return {
        "projected": draw_projected(jax.random.fold_in(jax.random.fold_in(key_list[6], part), 71), part),
        "assignment": draw_assignment(jax.random.fold_in(jax.random.fold_in(key_list[6], part), 71), part),
        "segments": jax.vmap(lambda own: jnp.searchsorted(jnp.cumsum(ragged_sizes(own, SEGS, ROW, MOST, 2)), jnp.arange(ROW), side="right"))(jax.random.split(part_keys[2], N_DP)).reshape((N_DP, ROW)).astype(jnp.int32),
        "advantage": normal_values(part_keys[3], (N_DP, SEGS), 1.0, 4.0, ((0, 4),), jnp.float32),
        "out_weight": normal_values(key_list[4], (HPAIR, 2, HS, D), (HEADS * HS) ** -0.5, 0.09375, ((0, 4), (1, 2), (3, 2))),
        "cotangent": normal_values(part_keys[5], (TOKENS, D), 1.0, 6.0, ((0, 4), (1, 2))),
    }


def attend_heads(queries, keys_all, values_all, seg_query, seg_key, offset):
    head_size = queries.shape[-1]
    scores = jnp.einsum('tkc,ukc->ktu', queries.astype(jnp.float32), keys_all.astype(jnp.float32), precision=lax.Precision.HIGHEST) * (1.0 / math.sqrt(head_size))
    pos_query = offset + jnp.arange(queries.shape[0], dtype=jnp.int32)
    pos_key = jnp.arange(keys_all.shape[0], dtype=jnp.int32)
    keep = (seg_query[:, None] == seg_key[None, :]) & (pos_key[None, :] <= pos_query[:, None])
    scores = jnp.where(keep[None], scores, -1e+30)
    rowmax = lax.optimization_barrier(jnp.max(scores, axis=-1, keepdims=True))
    expd = jnp.where(keep[None], jnp.exp(scores - rowmax), 0.0)
    probs = (expd / lax.optimization_barrier(jnp.sum(expd, axis=-1, keepdims=True))).astype(jnp.bfloat16)
    attended = jnp.einsum('ktu,ukc->tkc', probs.astype(jnp.float32), values_all.astype(jnp.float32), precision=lax.Precision.HIGHEST)
    return attended.astype(jnp.bfloat16)

def reference(projected, assignment, segments, advantage, out_weight, cotangent):
    count_all = N_DP * NBLK
    flat = jnp.transpose(assignment, (1, 0, 2)).reshape(N_SEQ, count_all)
    source = jnp.arange(count_all, dtype=jnp.int32)
    order = jnp.argsort(flat * count_all + source[None, :], axis=1).astype(jnp.int32)
    blocks = projected.reshape(3, N_DP, N_SEQ, NBLK, BLK, HPAIR, 2, HS)
    blocks = jnp.transpose(blocks, (0, 2, 1, 3, 4, 5, 6, 7)).reshape(3, N_SEQ, count_all, BLK, HPAIR, 2, HS)
    moved = jax.vmap(lambda block_set, picks: block_set[:, picks], in_axes=(1, 0), out_axes=1)(blocks, order)
    moved = moved.reshape(3, N_SEQ, N_DP, NBLK, BLK, HPAIR, 2, HS)
    trained = jnp.transpose(moved, (0, 2, 1, 3, 4, 5, 6, 7)).reshape(3, N_DP, ROW, HEADS, HS)
    weight_wide = out_weight.astype(jnp.float32)
    labels = jnp.arange(SEGS, dtype=jnp.int32)

    def one_row(total_grad, inputs):
        queries, keys_all, values_all, seg_row, adv_row, cot_row = inputs
        attended = attend_heads(queries, keys_all, values_all, seg_row, seg_row, 0)
        att_wide = attended.astype(jnp.float32).reshape(ROW, HPAIR, 2, HS)
        partial_value = jnp.einsum('tkpc,kpcn->ptn', att_wide, weight_wide, precision=lax.Precision.HIGHEST)
        partial_value = lax.optimization_barrier(partial_value.astype(jnp.bfloat16)).astype(jnp.float32)
        mixed_row = (partial_value[0] + partial_value[1]).astype(jnp.bfloat16)
        member = (seg_row[:, None] == labels[None, :]).astype(jnp.float32)
        sizes_tok = lax.optimization_barrier(jnp.sum(member * lax.optimization_barrier(jnp.sum(member, axis=0))[None, :], axis=1))
        adv_tok = lax.optimization_barrier(jnp.sum(member * adv_row[None, :], axis=1))
        scaled = (cot_row.astype(jnp.float32) * (adv_tok / sizes_tok)[:, None]).astype(jnp.bfloat16)
        row_grad = jnp.einsum('tkpc,tn->kpcn', att_wide, scaled.astype(jnp.float32), precision=lax.Precision.HIGHEST)
        row_grad = lax.optimization_barrier(row_grad.astype(jnp.bfloat16)).astype(jnp.float32)
        return (total_grad + row_grad, mixed_row)
    start_grad = jnp.zeros((HPAIR, 2, HS, D), jnp.float32)
    weight_grad, mixed_rows = lax.scan(one_row, start_grad, (trained[0], trained[1], trained[2], segments, advantage, cotangent.reshape(N_DP, ROW, D)))
    return (mixed_rows.reshape(TOKENS, D), weight_grad)
```

```python
import functools
import math

import jax
import jax.numpy as jnp
from jax import lax
from jax.experimental import pallas as pl
from jax.experimental.pallas import tpu as pltpu
from jax.sharding import PartitionSpec as P

CAP = 2


def attend_heads(queries, keys_all, values_all, seg_query, seg_key):
    head_size = queries.shape[-1]
    scores = jnp.einsum("tkc,ukc->ktu", queries, keys_all, preferred_element_type=jnp.float32) * (
        1.0 / math.sqrt(head_size)
    )
    pos_query = jnp.arange(queries.shape[0], dtype=jnp.int32)
    pos_key = jnp.arange(keys_all.shape[0], dtype=jnp.int32)
    keep = (seg_query[:, None] == seg_key[None, :]) & (pos_key[None, :] <= pos_query[:, None])
    scores = jnp.where(keep[None], scores, -1e30)
    rowmax = jnp.max(scores, axis=-1, keepdims=True)
    expd = jnp.where(keep[None], jnp.exp(scores - rowmax), 0.0)
    probs = (expd / jnp.sum(expd, axis=-1, keepdims=True)).astype(jnp.bfloat16)
    attended = jnp.einsum("ktu,ukc->tkc", probs, values_all, preferred_element_type=jnp.float32)
    return attended.astype(jnp.bfloat16)


def token_weight(seg_row, adv_row):
    labels = jnp.arange(adv_row.shape[0], dtype=jnp.int32)
    member_seg = (seg_row[:, None] == labels[None, :]).astype(jnp.float32)
    sizes_tok = jnp.sum(member_seg * jnp.sum(member_seg, axis=0)[None, :], axis=1)
    adv_tok = jnp.sum(member_seg * adv_row[None, :], axis=1)
    return adv_tok / sizes_tok


def body_rows(projected, assignment, segments, advantage, out_weight, cotangent):
    shards = lax.axis_size("dp")
    tok_rows = projected.shape[1]
    head_count = projected.shape[2]
    head_size = projected.shape[4]
    block_len = tok_rows // shards
    out_cols = out_weight.shape[3]
    blocks = jnp.transpose(
        projected.reshape(3, shards, block_len, head_count, head_size), (1, 0, 2, 3, 4)
    )
    targets = assignment.reshape(shards)
    member = (targets[:, None] == jnp.arange(shards, dtype=jnp.int32)[None, :]).astype(jnp.int32)
    ranks = jnp.sum((jnp.cumsum(member, axis=0) - member) * member, axis=1)
    counts = jnp.sum(member, axis=0).reshape(shards, 1)
    outgoing = jnp.zeros((shards, CAP, 3, block_len, head_count, head_size), projected.dtype)
    outgoing = outgoing.at[targets, ranks].set(blocks)
    incoming, arrived = (
        lax.all_to_all(outgoing, "dp", split_axis=0, concat_axis=0, tiled=True),
        lax.all_to_all(counts, "dp", split_axis=0, concat_axis=0, tiled=True),
    )
    arrived = arrived.reshape(shards)
    firsts = jnp.cumsum(arrived) - arrived
    slots = jnp.arange(CAP, dtype=jnp.int32)
    places = jnp.where(slots[None, :] < arrived[:, None], firsts[:, None] + slots[None, :], shards)
    packed = jnp.zeros((shards, 3, block_len, head_count, head_size), projected.dtype)
    packed = packed.at[places.reshape(-1)].set(
        incoming.reshape(shards * CAP, 3, block_len, head_count, head_size), mode="drop"
    )
    local = jnp.transpose(packed, (1, 0, 2, 3, 4)).reshape(3, tok_rows, head_count, head_size)
    seg_row = segments[0]
    weight = token_weight(seg_row, advantage[0])
    scaled = (cotangent.astype(jnp.float32) * weight[:, None]).astype(jnp.bfloat16)
    gathered = lax.all_gather(out_weight, "dp", axis=0, tiled=True)
    weight_rows = gathered.reshape(head_count, head_size, out_cols)
    switched = lax.all_to_all(local, "seq", split_axis=2, concat_axis=1, tiled=True)
    attended = attend_heads(switched[0], switched[1], switched[2], seg_row, seg_row)
    piece = lax.all_gather(attended, "seq", axis=1, tiled=True)
    total = jnp.einsum("tkc,kcn->tn", piece, weight_rows, preferred_element_type=jnp.float32)
    term = jnp.einsum("tkc,tn->kcn", piece, scaled, preferred_element_type=jnp.float32)
    mixed = lax.psum_scatter(total.astype(jnp.bfloat16), "head", scatter_dimension=1, tiled=True)
    weight_grad = lax.psum_scatter(
        term.reshape(head_count, 1, head_size, out_cols).astype(jnp.bfloat16),
        "dp",
        scatter_dimension=0,
        tiled=True,
    ).astype(jnp.float32)
    return (mixed, weight_grad)


def attention_kernel(rows, nseq, nblk, blk, assign, seg_lane, seg_sub, recv, out, packed, order):
    heads, head_size = recv.shape[2], recv.shape[4]
    row_len = seg_lane.shape[1]
    per_shard = row_len // nseq // blk
    for s in range(nseq):
        counts = [jnp.int32(0)] * rows
        for o in range(rows):
            for b in range(nblk):
                target = assign[o * nseq + s, b]
                slot = counts[0]
                for r in range(1, rows):
                    slot = jnp.where(target == r, counts[r], slot)
                order[(target * nseq + s) * per_shard + slot] = o * nblk + b
                counts = [counts[r] + (target == r).astype(jnp.int32) for r in range(rows)]
    pos_query = lax.broadcasted_iota(jnp.int32, (row_len, row_len), 0)
    pos_key = lax.broadcasted_iota(jnp.int32, (row_len, row_len), 1)
    causal = pos_key <= pos_query
    scale = 1.0 / math.sqrt(head_size)
    for r in range(rows):
        keep = causal & (seg_sub[:, r : r + 1] == seg_lane[r : r + 1, :])
        for s in range(nseq):
            for slot in range(per_shard):
                source = order[(r * nseq + s) * per_shard + slot]
                owner, block = lax.div(source, nblk), lax.rem(source, nblk)
                first = pl.multiple_of(block * blk, blk)
                place = (s * per_shard + slot) * blk
                packed[:, :, place : place + blk, :] = recv[owner * nseq + s, :, :, pl.ds(first, blk), :]
        for h in range(heads):
            scores = lax.dot_general(
                packed[0, h], packed[1, h], (((1,), (1,)), ((), ())), preferred_element_type=jnp.float32
            ) * scale
            scores = jnp.where(keep, scores, -1e30)
            rowmax = jnp.max(scores, axis=-1, keepdims=True)
            expd = jnp.where(keep, jnp.exp(scores - rowmax), 0.0)
            probs = (expd / jnp.sum(expd, axis=-1, keepdims=True)).astype(jnp.bfloat16)
            attended = jnp.dot(probs, packed[2, h], preferred_element_type=jnp.float32)
            out[r * row_len : (r + 1) * row_len, h * head_size : (h + 1) * head_size] = attended.astype(
                jnp.bfloat16
            )


def attend_rows(recv, assign, segs, nblk):
    peers, _, heads, tokens, head_size = recv.shape
    rows, row_len = segs.shape
    nseq = peers // rows
    return pl.pallas_call(
        functools.partial(attention_kernel, rows, nseq, nblk, tokens // nblk),
        out_shape=jax.ShapeDtypeStruct((rows * row_len, heads * head_size), jnp.bfloat16),
        in_specs=[
            pl.BlockSpec(memory_space=pltpu.SMEM),
            pl.BlockSpec(memory_space=pltpu.VMEM),
            pl.BlockSpec(memory_space=pltpu.VMEM),
            pl.BlockSpec(memory_space=pltpu.VMEM),
        ],
        out_specs=pl.BlockSpec(memory_space=pltpu.VMEM),
        scratch_shapes=[
            pltpu.VMEM((3, heads, row_len, head_size), jnp.bfloat16),
            pltpu.SMEM((rows * nblk * nseq,), jnp.int32),
        ],
        compiler_params=pltpu.CompilerParams(vmem_limit_bytes=32 << 20),
        cost_estimate=pl.CostEstimate(
            flops=4 * rows * heads * row_len * row_len * head_size,
            bytes_accessed=recv.size * 2 + rows * row_len * heads * head_size * 2,
            transcendentals=rows * heads * row_len * row_len,
        ),
        name="attend_rows",
    )(assign, segs, segs.T, recv)


def swap(x, axis):
    return lax.ppermute(x, axis, [(0, 1), (1, 0)])


def body_heads(projected, assignment, segments, advantage, out_weight, cotangent):
    ndp, nseq = lax.axis_size("dp"), lax.axis_size("seq")
    me, my_seq, my_head = lax.axis_index("dp"), lax.axis_index("seq"), lax.axis_index("head")
    tokens, pairs, head_size = projected.shape[1], projected.shape[2], projected.shape[4]
    nblk = assignment.shape[2]
    row_len = segments.shape[1]
    mine = pairs // (ndp * nseq)
    cols = out_weight.shape[3]
    half = cols // 2
    width = mine * head_size

    small = jnp.concatenate([assignment.reshape(nblk), segments.reshape(row_len)])
    small = jnp.broadcast_to(small[None], (ndp * nseq, nblk + row_len))
    small = lax.all_to_all(small, ("dp", "seq"), split_axis=0, concat_axis=0, tiled=True)
    assign, segs = small[:, :nblk], small[::nseq, nblk:]

    sent = projected.reshape(3, tokens, ndp * nseq, mine, head_size).transpose(2, 0, 3, 1, 4)
    recv = lax.all_to_all(sent, ("dp", "seq"), split_axis=0, concat_axis=0, tiled=True)

    weight = token_weight(segments[0], advantage[0])
    own_cols = lax.dynamic_slice_in_dim(cotangent, my_head * half, half, 1)
    scaled = (own_cols.astype(jnp.float32) * weight[:, None]).astype(jnp.bfloat16)

    rows_w = out_weight.reshape(nseq * width, cols)
    keep_w = lax.dynamic_slice_in_dim(rows_w, my_head * half, half, 1)
    other_w = swap(lax.dynamic_slice_in_dim(rows_w, (1 - my_head) * half, half, 1), "head")

    recv, scaled = lax.optimization_barrier((recv, scaled))
    att = attend_rows(recv, assign, segs, nblk)

    def both(x):
        other = swap(x, "head")
        return jnp.where(my_head == 0, jnp.concatenate([x, other], 1), jnp.concatenate([other, x], 1))

    pieces = [scaled] + [
        lax.ppermute(scaled, "dp", [(i, i ^ k) for i in range(ndp)]) for k in range(1, ndp)
    ]
    pieces = [both(x) for x in pieces]

    att_seq = swap(att, "seq")
    att_head = swap(att, "head")
    att_diag = swap(att_seq, "head")

    def slab(w, s):
        return lax.dynamic_slice_in_dim(w, s * width, width, 0)

    def rows_of(x, k):
        return lax.dynamic_slice_in_dim(x, (me ^ k) * row_len, row_len, 0)

    weights = jnp.concatenate(
        [slab(keep_w, my_seq), slab(other_w, my_seq), slab(keep_w, 1 - my_seq), slab(other_w, 1 - my_seq)], 0
    )
    terms = []
    for k in reversed(range(ndp)):
        row = jnp.concatenate([rows_of(x, k) for x in (att, att_head, att_seq, att_diag)], 1)
        total = jnp.dot(row, weights, preferred_element_type=jnp.float32)
        if k:
            total = lax.ppermute(total.astype(jnp.bfloat16), "dp", [(i, i ^ k) for i in range(ndp)])
        terms.append(total.astype(jnp.float32))
    mixed = functools.reduce(jnp.add, terms).astype(jnp.bfloat16)

    pair = jnp.where(my_seq == 0, jnp.concatenate([att, att_seq], 1), jnp.concatenate([att_seq, att], 1))
    left = jnp.concatenate([rows_of(pair, k) for k in range(ndp)], 0)
    grad = lax.dot_general(
        left, jnp.concatenate(pieces, 0), (((0,), (0,)), ((), ())), preferred_element_type=jnp.float32
    )
    return mixed, grad.reshape(nseq * mine, 1, head_size, cols)


def solution(mesh):
    placed = (
        P(None, ("groups", "dp", "seq"), None, "head", None),
        P(("groups", "dp"), "seq", None),
        P(("groups", "dp"), None),
        P(("groups", "dp"), None),
        P("dp", "head", None, "seq"),
        P(("groups", "dp"), "seq"),
    )

    def body(projected, *rest):
        ndp, nseq = mesh.shape["dp"], mesh.shape["seq"]
        fits = projected.shape[2] % (ndp * nseq) == 0 and (ndp, nseq) == (4, 2)
        return (body_heads if fits else body_rows)(projected, *rest)

    return jax.shard_map(
        body,
        mesh=mesh,
        in_specs=placed,
        out_specs=(P(("groups", "dp"), ("seq", "head")), P(("groups", "dp"), "head", None, "seq")),
        check_vma=False,
    )
```

```python
import functools
import math

import jax
import jax.numpy as jnp
from jax import lax
from jax.experimental import pallas as pl
from jax.experimental.pallas import tpu as pltpu
from jax.sharding import PartitionSpec as P

CAP = 2
SHORT = pl.CostEstimate(flops=1000, bytes_accessed=1000, transcendentals=0)
ROW_AT = ((3, 2, 1, 0), (3, 2, 0, 1), (0, 1, 3, 2), (0, 1, 2, 3))
PLACE_OF = ((3, 2, 1, 0), (2, 3, 1, 0), (0, 1, 3, 2), (0, 1, 2, 3))


def attend_heads(queries, keys_all, values_all, seg_query, seg_key):
    head_size = queries.shape[-1]
    scores = jnp.einsum("tkc,ukc->ktu", queries, keys_all, preferred_element_type=jnp.float32) * (
        1.0 / math.sqrt(head_size)
    )
    pos_query = jnp.arange(queries.shape[0], dtype=jnp.int32)
    pos_key = jnp.arange(keys_all.shape[0], dtype=jnp.int32)
    keep = (seg_query[:, None] == seg_key[None, :]) & (pos_key[None, :] <= pos_query[:, None])
    scores = jnp.where(keep[None], scores, -1e30)
    rowmax = jnp.max(scores, axis=-1, keepdims=True)
    expd = jnp.where(keep[None], jnp.exp(scores - rowmax), 0.0)
    probs = (expd / jnp.sum(expd, axis=-1, keepdims=True)).astype(jnp.bfloat16)
    attended = jnp.einsum("ktu,ukc->tkc", probs, values_all, preferred_element_type=jnp.float32)
    return attended.astype(jnp.bfloat16)


def token_weight(seg_row, adv_row):
    labels = jnp.arange(adv_row.shape[0], dtype=jnp.int32)
    member_seg = (seg_row[:, None] == labels[None, :]).astype(jnp.float32)
    sizes_tok = jnp.sum(member_seg * jnp.sum(member_seg, axis=0)[None, :], axis=1)
    adv_tok = jnp.sum(member_seg * adv_row[None, :], axis=1)
    return adv_tok / sizes_tok


def body_rows(projected, assignment, segments, advantage, out_weight, cotangent):
    shards = lax.axis_size("dp")
    tok_rows = projected.shape[1]
    head_count = projected.shape[2]
    head_size = projected.shape[4]
    block_len = tok_rows // shards
    out_cols = out_weight.shape[3]
    blocks = jnp.transpose(
        projected.reshape(3, shards, block_len, head_count, head_size), (1, 0, 2, 3, 4)
    )
    targets = assignment.reshape(shards)
    member = (targets[:, None] == jnp.arange(shards, dtype=jnp.int32)[None, :]).astype(jnp.int32)
    ranks = jnp.sum((jnp.cumsum(member, axis=0) - member) * member, axis=1)
    counts = jnp.sum(member, axis=0).reshape(shards, 1)
    outgoing = jnp.zeros((shards, CAP, 3, block_len, head_count, head_size), projected.dtype)
    outgoing = outgoing.at[targets, ranks].set(blocks)
    incoming, arrived = (
        lax.all_to_all(outgoing, "dp", split_axis=0, concat_axis=0, tiled=True),
        lax.all_to_all(counts, "dp", split_axis=0, concat_axis=0, tiled=True),
    )
    arrived = arrived.reshape(shards)
    firsts = jnp.cumsum(arrived) - arrived
    slots = jnp.arange(CAP, dtype=jnp.int32)
    places = jnp.where(slots[None, :] < arrived[:, None], firsts[:, None] + slots[None, :], shards)
    packed = jnp.zeros((shards, 3, block_len, head_count, head_size), projected.dtype)
    packed = packed.at[places.reshape(-1)].set(
        incoming.reshape(shards * CAP, 3, block_len, head_count, head_size), mode="drop"
    )
    local = jnp.transpose(packed, (1, 0, 2, 3, 4)).reshape(3, tok_rows, head_count, head_size)
    seg_row = segments[0]
    weight = token_weight(seg_row, advantage[0])
    scaled = (cotangent.astype(jnp.float32) * weight[:, None]).astype(jnp.bfloat16)
    gathered = lax.all_gather(out_weight, "dp", axis=0, tiled=True)
    weight_rows = gathered.reshape(head_count, head_size, out_cols)
    switched = lax.all_to_all(local, "seq", split_axis=2, concat_axis=1, tiled=True)
    attended = attend_heads(switched[0], switched[1], switched[2], seg_row, seg_row)
    piece = lax.all_gather(attended, "seq", axis=1, tiled=True)
    total = jnp.einsum("tkc,kcn->tn", piece, weight_rows, preferred_element_type=jnp.float32)
    term = jnp.einsum("tkc,tn->kcn", piece, scaled, preferred_element_type=jnp.float32)
    mixed = lax.psum_scatter(total.astype(jnp.bfloat16), "head", scatter_dimension=1, tiled=True)
    weight_grad = lax.psum_scatter(
        term.reshape(head_count, 1, head_size, out_cols).astype(jnp.bfloat16),
        "dp",
        scatter_dimension=0,
        tiled=True,
    ).astype(jnp.float32)
    return (mixed, weight_grad)


def attention_kernel(places, labels, nblk, blk, assign, row_at, place_of, segs, recv, out, packed, order):
    heads, row_len, head_size = packed.shape[1:]
    tokens = nblk * blk
    rows = segs.shape[0]
    nseq = recv.shape[0] // rows
    per_shard = row_len // nseq // blk
    for s in range(nseq):
        counts = [jnp.int32(0)] * rows
        for o in range(rows):
            for b in range(nblk):
                target = place_of[assign[o * nseq + s, b]]
                slot = counts[0]
                for r in range(1, rows):
                    slot = jnp.where(target == r, counts[r], slot)
                order[(target * nseq + s) * per_shard + slot] = o * nblk + b
                counts = [counts[r] + (target == r).astype(jnp.int32) for r in range(rows)]
    pos_query = lax.broadcasted_iota(jnp.int32, (row_len, 1), 0)
    pos_key = lax.broadcasted_iota(jnp.int32, (1, row_len), 1)
    causal = pos_key <= pos_query
    scale = 1.0 / math.sqrt(head_size)
    for i, r in enumerate(places):
        ids = segs[pl.ds(row_at[r], 1), :]
        query_id, key_id = jnp.zeros_like(pos_query), ids
        for label in range(1, labels):
            lower = jnp.sum((ids < label).astype(jnp.int32), axis=1, keepdims=True)
            query_id = query_id + (pos_query >= lower).astype(jnp.int32)
        keep = causal & (query_id == key_id)
        for s in range(nseq):
            for slot in range(per_shard):
                source = order[(r * nseq + s) * per_shard + slot]
                owner, block = lax.div(source, nblk), lax.rem(source, nblk)
                first = pl.multiple_of(block * blk, blk)
                place = (s * per_shard + slot) * blk
                for c in range(3):
                    for h in range(heads):
                        packed[c, h, place : place + blk, :] = recv[
                            owner * nseq + s, pl.ds((c * heads + h) * tokens + first, blk), :
                        ]
        for h in range(heads):
            scores = lax.dot_general(
                packed[0, h], packed[1, h], (((1,), (1,)), ((), ())), preferred_element_type=jnp.float32
            ) * scale
            scores = jnp.where(keep, scores, -1e30)
            rowmax = jnp.max(scores, axis=-1, keepdims=True)
            expd = jnp.where(keep, jnp.exp(scores - rowmax), 0.0)
            probs = (expd / jnp.sum(expd, axis=-1, keepdims=True)).astype(jnp.bfloat16)
            attended = jnp.dot(probs, packed[2, h], preferred_element_type=jnp.float32)
            out[i * row_len : (i + 1) * row_len, h * head_size : (h + 1) * head_size] = attended.astype(
                jnp.bfloat16
            )


def attend_rows(places, recv, assign, row_at, place_of, segs, labels, heads):
    head_size = recv.shape[2]
    rows, row_len = segs.shape
    nblk = assign.shape[1]
    tokens = row_len * rows // recv.shape[0]
    count = len(places)
    smem, vmem = pl.BlockSpec(memory_space=pltpu.SMEM), pl.BlockSpec(memory_space=pltpu.VMEM)
    return pl.pallas_call(
        functools.partial(attention_kernel, places, labels, nblk, tokens // nblk),
        out_shape=jax.ShapeDtypeStruct((count * row_len, heads * head_size), jnp.bfloat16),
        in_specs=[smem, smem, smem, vmem, vmem],
        out_specs=vmem,
        scratch_shapes=[
            pltpu.VMEM((3, heads, row_len, head_size), jnp.bfloat16),
            pltpu.SMEM((recv.shape[0] * nblk,), jnp.int32),
        ],
        compiler_params=pltpu.CompilerParams(vmem_limit_bytes=32 << 20),
        cost_estimate=SHORT,
        name="attend_rows",
    )(assign, row_at, place_of, segs, recv)


def gradient_kernel(place, far, near, far_seq, near_seq, *refs):
    own, other, out, turned = refs[:4], refs[4:8], refs[8], refs[9]
    width = far.shape[1]
    row_len = own[0].shape[0]

    @pl.when((pl.program_id(0) == 0) & (pl.program_id(1) == 0))
    def _():
        for s, parts in enumerate(((far, near), (far_seq, near_seq))):
            first = pl.multiple_of(width * (place[0] if s == 0 else 1 - place[0]), width)
            for i, part in enumerate(parts):
                turned[pl.ds(first, width), 2 * i * row_len : 2 * (i + 1) * row_len] = part[...].T

    for side, group in enumerate((own, other)):

        @pl.when(pl.program_id(0) == side)
        def _():
            rows = jnp.concatenate([x[...] for x in group], 0)
            out[...] = jnp.dot(turned[...], rows, preferred_element_type=jnp.float32)


def weight_gradient(att, att_seq, pieces, others, my_seq, my_head):
    width = att[0].shape[1]
    row_len, half = pieces[0].shape
    tile = math.gcd(half, 640)
    tiles = half // tile
    whole = pl.BlockSpec(att[0].shape, lambda side, t, place: (0, 0))
    own = pl.BlockSpec((row_len, tile), lambda side, t, place: (0, jnp.where(side == 0, t, tiles - 1)))
    other = pl.BlockSpec((row_len, tile), lambda side, t, place: (0, jnp.where(side == 0, 0, t)))
    out = pl.BlockSpec(
        (2 * width, tile), lambda side, t, place: (0, jnp.where(side == 0, place[1], 1 - place[1]) * tiles + t)
    )
    return pl.pallas_call(
        gradient_kernel,
        out_shape=jax.ShapeDtypeStruct((2 * width, 2 * half), jnp.float32),
        grid_spec=pltpu.PrefetchScalarGridSpec(
            num_scalar_prefetch=1,
            grid=(2, tiles),
            in_specs=[whole] * 4 + [own] * 4 + [other] * 4,
            out_specs=out,
            scratch_shapes=[pltpu.VMEM((2 * width, 4 * row_len), jnp.bfloat16)],
        ),
        compiler_params=pltpu.CompilerParams(vmem_limit_bytes=40 << 20),
        cost_estimate=SHORT,
        name="weight_gradient",
    )(jnp.stack([my_seq, my_head]).astype(jnp.int32), *att, *att_seq, *pieces, *others)


def swap(x, axis, name="swap"):
    with jax.named_scope(name):
        return lax.ppermute(x, axis, [(0, 1), (1, 0)])


def after(x, *first):
    return lax.optimization_barrier((x, *first))[0]


def add(x, y):
    return (x.astype(jnp.float32) + y.astype(jnp.float32)).astype(jnp.bfloat16)


def body_heads(projected, assignment, segments, advantage, out_weight, cotangent):
    ndp, nseq = lax.axis_size("dp"), lax.axis_size("seq")
    me, my_seq, my_head = lax.axis_index("dp"), lax.axis_index("seq"), lax.axis_index("head")
    tokens, pairs, head_size = projected.shape[1], projected.shape[2], projected.shape[4]
    nblk = assignment.shape[2]
    row_len = segments.shape[1]
    peers = ndp * nseq
    mine = pairs // peers
    cols = out_weight.shape[3]
    half = cols // 2
    width = mine * head_size

    sent = projected.reshape(3, tokens, peers, mine, head_size).transpose(2, 0, 3, 1, 4)
    sent = sent.reshape(peers, 3 * mine * tokens, head_size)
    small = [segments[0], assignment.reshape(nblk), jnp.zeros((16 * head_size - row_len - nblk,), jnp.int32)]
    small = jnp.concatenate(small).astype(jnp.bfloat16).reshape(1, 16, head_size)
    sent = jnp.concatenate([sent, jnp.broadcast_to(small, (peers, 16, head_size))], 1)
    recv = lax.all_to_all(sent, ("dp", "seq"), split_axis=0, concat_axis=0, tiled=True)
    small = recv[:, 3 * mine * tokens :].astype(jnp.int32).reshape(peers, 16 * head_size)
    assign, segs = small[:, row_len : row_len + nblk], small[::nseq, :row_len]

    weight = token_weight(segments[0], advantage[0])
    own_cols = lax.dynamic_slice_in_dim(cotangent, my_head * half, half, 1)
    scaled = (own_cols.astype(jnp.float32) * weight[:, None]).astype(jnp.bfloat16)

    rows_w = out_weight.reshape(nseq * width, cols)
    keep_w = lax.dynamic_slice_in_dim(rows_w, my_head * half, half, 1)
    other_w = swap(lax.dynamic_slice_in_dim(rows_w, (1 - my_head) * half, half, 1), "head")

    def slab(w, s):
        return lax.dynamic_slice_in_dim(w, s * width, width, 0)

    weights = jnp.concatenate(
        [slab(keep_w, my_seq), slab(other_w, my_seq), slab(keep_w, 1 - my_seq), slab(other_w, 1 - my_seq)], 0
    )

    recv, assign, segs, scaled, weights = lax.optimization_barrier((recv, assign, segs, scaled, weights))

    row_at = jnp.asarray(ROW_AT, jnp.int32)[me]
    place_of = jnp.asarray(PLACE_OF, jnp.int32)[me]
    attend = functools.partial(
        attend_rows, assign=assign, row_at=row_at, place_of=place_of, segs=segs, labels=advantage.shape[1], heads=mine
    )
    across, middle = ((0, 1), (1, 0), (2, 3), (3, 2)), ((1, 2), (2, 1))

    def send(x, perm, name):
        with jax.named_scope(name):
            return lax.ppermute(x, "dp", perm)

    def project(att, att_head, att_seq, att_diag):
        rows = jnp.concatenate([att, att_head, att_seq, att_diag], 1)
        return jnp.dot(rows, weights, preferred_element_type=jnp.float32).astype(jnp.bfloat16)

    inner = (me == 1) | (me == 2)

    from_2, mid_1 = send(scaled, across, "swap_0"), send(scaled, middle, "mid_0")

    far = attend((0, 1), recv)
    far_seq, far_head = swap(far, "seq", "far_seq"), swap(far, "head", "far_head")
    near = after(attend((2, 3), recv), far_seq)
    far_seq, from_2, mid_1 = lax.optimization_barrier((far_seq, from_2, mid_1))
    far_diag = swap(far_seq, "head", "far_diag")
    near_seq, near_head = swap(near, "seq", "near_seq"), swap(near, "head", "near_head")
    far_terms = project(far, far_head, far_seq, far_diag)
    first, second = far_terms[:row_len], far_terms[row_len:]
    near_diag = swap(near_seq, "head", "near_diag")
    near_terms = project(near, near_head, near_seq, near_diag)
    third, own = near_terms[:row_len], near_terms[row_len:]

    swapped_1 = send(jnp.where(inner, mid_1, first), across, "swap_1")
    mid_0 = send(after(from_2, first), middle, "mid_1")
    swapped_1, mid_0, second, third = lax.optimization_barrier((swapped_1, mid_0, second, third))
    swapped_2 = send(jnp.where(inner, mid_0, second), across, "swap_2")
    crossed_2 = send(add(first, swapped_1), middle, "mid_2")
    swapped_2, crossed_2 = lax.optimization_barrier((swapped_2, crossed_2))
    swapped_3 = send(add(third, crossed_2), across, "swap_3")
    crossed_3 = send(add(second, swapped_2), middle, "mid_3")

    pieces = [jnp.where(inner, mid_0, swapped_2), jnp.where(inner, mid_1, swapped_1), from_2, scaled]
    others = [swap(x, "head", f"piece_{i}") for i, x in enumerate(pieces)]
    grad = weight_gradient((far, near), (far_seq, near_seq), pieces, others, my_seq, my_head)
    swapped_3, crossed_3, grad = lax.optimization_barrier((swapped_3, crossed_3, grad))
    mixed = own.astype(jnp.float32) + swapped_3.astype(jnp.float32) + crossed_3.astype(jnp.float32)
    return mixed.astype(jnp.bfloat16), grad.reshape(nseq * mine, 1, head_size, cols)


def solution(mesh):
    placed = (
        P(None, ("groups", "dp", "seq"), None, "head", None),
        P(("groups", "dp"), "seq", None),
        P(("groups", "dp"), None),
        P(("groups", "dp"), None),
        P("dp", "head", None, "seq"),
        P(("groups", "dp"), "seq"),
    )

    def body(projected, *rest):
        ndp, nseq = mesh.shape["dp"], mesh.shape["seq"]
        fits = projected.shape[2] % (ndp * nseq) == 0 and (ndp, nseq) == (4, 2)
        return (body_heads if fits else body_rows)(projected, *rest)

    return jax.shard_map(
        body,
        mesh=mesh,
        in_specs=placed,
        out_specs=(P(("groups", "dp"), ("seq", "head")), P(("groups", "dp"), "head", None, "seq")),
        check_vma=False,
    )
```

```python
import functools
import math

import jax
import jax.numpy as jnp
from jax import lax
from jax.experimental import pallas as pl
from jax.experimental.pallas import tpu as pltpu
from jax.sharding import PartitionSpec as P

CAP = 2
SHORT = pl.CostEstimate(flops=1000, bytes_accessed=1000, transcendentals=0)
ROW_AT = ((3, 2, 1, 0), (3, 2, 0, 1), (0, 1, 3, 2), (0, 1, 2, 3))
PLACE_OF = ((3, 2, 1, 0), (2, 3, 1, 0), (0, 1, 3, 2), (0, 1, 2, 3))


def attend_heads(queries, keys_all, values_all, seg_query, seg_key):
    head_size = queries.shape[-1]
    scores = jnp.einsum("tkc,ukc->ktu", queries, keys_all, preferred_element_type=jnp.float32) * (
        1.0 / math.sqrt(head_size)
    )
    pos_query = jnp.arange(queries.shape[0], dtype=jnp.int32)
    pos_key = jnp.arange(keys_all.shape[0], dtype=jnp.int32)
    keep = (seg_query[:, None] == seg_key[None, :]) & (pos_key[None, :] <= pos_query[:, None])
    scores = jnp.where(keep[None], scores, -1e30)
    rowmax = jnp.max(scores, axis=-1, keepdims=True)
    expd = jnp.where(keep[None], jnp.exp(scores - rowmax), 0.0)
    probs = (expd / jnp.sum(expd, axis=-1, keepdims=True)).astype(jnp.bfloat16)
    attended = jnp.einsum("ktu,ukc->tkc", probs, values_all, preferred_element_type=jnp.float32)
    return attended.astype(jnp.bfloat16)


def token_weight(seg_row, adv_row):
    labels = jnp.arange(adv_row.shape[0], dtype=jnp.int32)
    member_seg = (seg_row[:, None] == labels[None, :]).astype(jnp.float32)
    sizes_tok = jnp.sum(member_seg * jnp.sum(member_seg, axis=0)[None, :], axis=1)
    adv_tok = jnp.sum(member_seg * adv_row[None, :], axis=1)
    return adv_tok / sizes_tok


def body_rows(projected, assignment, segments, advantage, out_weight, cotangent):
    shards = lax.axis_size("dp")
    tok_rows = projected.shape[1]
    head_count = projected.shape[2]
    head_size = projected.shape[4]
    block_len = tok_rows // shards
    out_cols = out_weight.shape[3]
    blocks = jnp.transpose(
        projected.reshape(3, shards, block_len, head_count, head_size), (1, 0, 2, 3, 4)
    )
    targets = assignment.reshape(shards)
    member = (targets[:, None] == jnp.arange(shards, dtype=jnp.int32)[None, :]).astype(jnp.int32)
    ranks = jnp.sum((jnp.cumsum(member, axis=0) - member) * member, axis=1)
    counts = jnp.sum(member, axis=0).reshape(shards, 1)
    outgoing = jnp.zeros((shards, CAP, 3, block_len, head_count, head_size), projected.dtype)
    outgoing = outgoing.at[targets, ranks].set(blocks)
    incoming, arrived = (
        lax.all_to_all(outgoing, "dp", split_axis=0, concat_axis=0, tiled=True),
        lax.all_to_all(counts, "dp", split_axis=0, concat_axis=0, tiled=True),
    )
    arrived = arrived.reshape(shards)
    firsts = jnp.cumsum(arrived) - arrived
    slots = jnp.arange(CAP, dtype=jnp.int32)
    places = jnp.where(slots[None, :] < arrived[:, None], firsts[:, None] + slots[None, :], shards)
    packed = jnp.zeros((shards, 3, block_len, head_count, head_size), projected.dtype)
    packed = packed.at[places.reshape(-1)].set(
        incoming.reshape(shards * CAP, 3, block_len, head_count, head_size), mode="drop"
    )
    local = jnp.transpose(packed, (1, 0, 2, 3, 4)).reshape(3, tok_rows, head_count, head_size)
    seg_row = segments[0]
    weight = token_weight(seg_row, advantage[0])
    scaled = (cotangent.astype(jnp.float32) * weight[:, None]).astype(jnp.bfloat16)
    gathered = lax.all_gather(out_weight, "dp", axis=0, tiled=True)
    weight_rows = gathered.reshape(head_count, head_size, out_cols)
    switched = lax.all_to_all(local, "seq", split_axis=2, concat_axis=1, tiled=True)
    attended = attend_heads(switched[0], switched[1], switched[2], seg_row, seg_row)
    piece = lax.all_gather(attended, "seq", axis=1, tiled=True)
    total = jnp.einsum("tkc,kcn->tn", piece, weight_rows, preferred_element_type=jnp.float32)
    term = jnp.einsum("tkc,tn->kcn", piece, scaled, preferred_element_type=jnp.float32)
    mixed = lax.psum_scatter(total.astype(jnp.bfloat16), "head", scatter_dimension=1, tiled=True)
    weight_grad = lax.psum_scatter(
        term.reshape(head_count, 1, head_size, out_cols).astype(jnp.bfloat16),
        "dp",
        scatter_dimension=0,
        tiled=True,
    ).astype(jnp.float32)
    return (mixed, weight_grad)


def attention_kernel(places, labels, nblk, blk, assign, row_at, place_of, segs, recv, out, packed, order):
    heads, row_len, head_size = packed.shape[1:]
    tokens = nblk * blk
    rows = segs.shape[0]
    nseq = recv.shape[0] // rows
    per_shard = row_len // nseq // blk
    for s in range(nseq):
        counts = [jnp.int32(0)] * rows
        for o in range(rows):
            for b in range(nblk):
                target = place_of[assign[o * nseq + s, b]]
                slot = counts[0]
                for r in range(1, rows):
                    slot = jnp.where(target == r, counts[r], slot)
                order[(target * nseq + s) * per_shard + slot] = o * nblk + b
                counts = [counts[r] + (target == r).astype(jnp.int32) for r in range(rows)]
    pos_query = lax.broadcasted_iota(jnp.int32, (row_len, 1), 0)
    pos_key = lax.broadcasted_iota(jnp.int32, (1, row_len), 1)
    causal = pos_key <= pos_query
    scale = 1.0 / math.sqrt(head_size)
    for i, r in enumerate(places):
        ids = segs[pl.ds(row_at[r], 1), :]
        query_id, key_id = jnp.zeros_like(pos_query), ids
        for label in range(1, labels):
            lower = jnp.sum((ids < label).astype(jnp.int32), axis=1, keepdims=True)
            query_id = query_id + (pos_query >= lower).astype(jnp.int32)
        keep = causal & (query_id == key_id)
        for s in range(nseq):
            for slot in range(per_shard):
                source = order[(r * nseq + s) * per_shard + slot]
                owner, block = lax.div(source, nblk), lax.rem(source, nblk)
                first = pl.multiple_of(block * blk, blk)
                place = (s * per_shard + slot) * blk
                for c in range(3):
                    for h in range(heads):
                        packed[c, h, place : place + blk, :] = recv[
                            owner * nseq + s, pl.ds((c * heads + h) * tokens + first, blk), :
                        ]
        for h in range(heads):
            scores = lax.dot_general(
                packed[0, h], packed[1, h], (((1,), (1,)), ((), ())), preferred_element_type=jnp.float32
            ) * scale
            scores = jnp.where(keep, scores, -1e30)
            rowmax = jnp.max(scores, axis=-1, keepdims=True)
            expd = jnp.where(keep, jnp.exp(scores - rowmax), 0.0)
            probs = (expd / jnp.sum(expd, axis=-1, keepdims=True)).astype(jnp.bfloat16)
            attended = jnp.dot(probs, packed[2, h], preferred_element_type=jnp.float32)
            out[i * row_len : (i + 1) * row_len, h * head_size : (h + 1) * head_size] = attended.astype(
                jnp.bfloat16
            )


def attend_rows(places, recv, assign, row_at, place_of, segs, labels, heads):
    head_size = recv.shape[2]
    rows, row_len = segs.shape
    nblk = assign.shape[1]
    tokens = row_len * rows // recv.shape[0]
    count = len(places)
    smem, vmem = pl.BlockSpec(memory_space=pltpu.SMEM), pl.BlockSpec(memory_space=pltpu.VMEM)
    return pl.pallas_call(
        functools.partial(attention_kernel, places, labels, nblk, tokens // nblk),
        out_shape=jax.ShapeDtypeStruct((count * row_len, heads * head_size), jnp.bfloat16),
        in_specs=[smem, smem, smem, vmem, vmem],
        out_specs=vmem,
        scratch_shapes=[
            pltpu.VMEM((3, heads, row_len, head_size), jnp.bfloat16),
            pltpu.SMEM((recv.shape[0] * nblk,), jnp.int32),
        ],
        compiler_params=pltpu.CompilerParams(vmem_limit_bytes=32 << 20),
        cost_estimate=SHORT,
        name="attend_rows",
    )(assign, row_at, place_of, segs, recv)


def project_kernel(*refs):
    parts, weights, outs = refs[:-3], refs[-3], refs[-2:]
    rows = jnp.concatenate([x[...] for x in parts], 1)
    total = jnp.dot(rows, weights[...], preferred_element_type=jnp.float32).astype(jnp.bfloat16)
    for i, out in enumerate(outs):
        out[...] = total[i * out.shape[0] : (i + 1) * out.shape[0]]


def project(parts, weights):
    tokens, width = parts[0].shape
    depth, half = weights.shape
    tile = math.gcd(half, 256)
    whole = pl.BlockSpec((tokens, width), lambda t: (0, 0))
    out = pl.BlockSpec((tokens // 2, tile), lambda t: (0, t))
    return pl.pallas_call(
        project_kernel,
        out_shape=[jax.ShapeDtypeStruct((tokens // 2, half), jnp.bfloat16)] * 2,
        grid=(half // tile,),
        in_specs=[whole] * len(parts) + [pl.BlockSpec((depth, tile), lambda t: (0, t))],
        out_specs=[out] * 2,
        compiler_params=pltpu.CompilerParams(vmem_limit_bytes=32 << 20),
        cost_estimate=SHORT,
        name="project",
    )(*parts, weights)


def gradient_kernel(place, far, near, far_seq, near_seq, *refs):
    own, other, out, turned = refs[:4], refs[4:8], refs[8], refs[9]
    width = far.shape[1]
    row_len = own[0].shape[0]

    @pl.when((pl.program_id(0) == 0) & (pl.program_id(1) == 0))
    def _():
        for s, parts in enumerate(((far, near), (far_seq, near_seq))):
            first = pl.multiple_of(width * (place[0] if s == 0 else 1 - place[0]), width)
            for i, part in enumerate(parts):
                turned[pl.ds(first, width), 2 * i * row_len : 2 * (i + 1) * row_len] = part[...].T

    for side, group in enumerate((own, other)):

        @pl.when(pl.program_id(0) == side)
        def _():
            rows = jnp.concatenate([x[...] for x in group], 0)
            out[...] = jnp.dot(turned[...], rows, preferred_element_type=jnp.float32)


def weight_gradient(att, att_seq, pieces, others, my_seq, my_head):
    width = att[0].shape[1]
    row_len, half = pieces[0].shape
    tile = math.gcd(half, 640)
    tiles = half // tile
    whole = pl.BlockSpec(att[0].shape, lambda side, t, place: (0, 0))
    own = pl.BlockSpec((row_len, tile), lambda side, t, place: (0, jnp.where(side == 0, t, tiles - 1)))
    other = pl.BlockSpec((row_len, tile), lambda side, t, place: (0, jnp.where(side == 0, 0, t)))
    out = pl.BlockSpec(
        (2 * width, tile), lambda side, t, place: (0, jnp.where(side == 0, place[1], 1 - place[1]) * tiles + t)
    )
    return pl.pallas_call(
        gradient_kernel,
        out_shape=jax.ShapeDtypeStruct((2 * width, 2 * half), jnp.float32),
        grid_spec=pltpu.PrefetchScalarGridSpec(
            num_scalar_prefetch=1,
            grid=(2, tiles),
            in_specs=[whole] * 4 + [own] * 4 + [other] * 4,
            out_specs=out,
            scratch_shapes=[pltpu.VMEM((2 * width, 4 * row_len), jnp.bfloat16)],
        ),
        compiler_params=pltpu.CompilerParams(vmem_limit_bytes=40 << 20),
        cost_estimate=SHORT,
        name="weight_gradient",
    )(jnp.stack([my_seq, my_head]).astype(jnp.int32), *att, *att_seq, *pieces, *others)


def swap(x, axis, name="swap"):
    with jax.named_scope(name):
        return lax.ppermute(x, axis, [(0, 1), (1, 0)])


def add(x, y):
    return (x.astype(jnp.float32) + y.astype(jnp.float32)).astype(jnp.bfloat16)


def body_heads(projected, assignment, segments, advantage, out_weight, cotangent):
    ndp, nseq = lax.axis_size("dp"), lax.axis_size("seq")
    me, my_seq, my_head = lax.axis_index("dp"), lax.axis_index("seq"), lax.axis_index("head")
    tokens, pairs, head_size = projected.shape[1], projected.shape[2], projected.shape[4]
    nblk = assignment.shape[2]
    row_len = segments.shape[1]
    peers = ndp * nseq
    mine = pairs // peers
    cols = out_weight.shape[3]
    half = cols // 2
    width = mine * head_size

    sent = projected.reshape(3, tokens, peers, mine, head_size).transpose(2, 0, 3, 1, 4)
    sent = sent.reshape(peers, 3 * mine * tokens, head_size)
    small = [segments[0], assignment.reshape(nblk), jnp.zeros((16 * head_size - row_len - nblk,), jnp.int32)]
    small = jnp.concatenate(small).astype(jnp.bfloat16).reshape(1, 16, head_size)
    sent = jnp.concatenate([sent, jnp.broadcast_to(small, (peers, 16, head_size))], 1)
    recv = lax.all_to_all(sent, ("dp", "seq"), split_axis=0, concat_axis=0, tiled=True)
    small = recv[:, 3 * mine * tokens :].astype(jnp.int32).reshape(peers, 16 * head_size)
    assign, segs = small[:, row_len : row_len + nblk], small[::nseq, :row_len]

    weight = token_weight(segments[0], advantage[0])
    own_cols = lax.dynamic_slice_in_dim(cotangent, my_head * half, half, 1)
    scaled = (own_cols.astype(jnp.float32) * weight[:, None]).astype(jnp.bfloat16)

    rows_w = out_weight.reshape(nseq * width, cols)
    keep_w = lax.dynamic_slice_in_dim(rows_w, my_head * half, half, 1)
    other_w = swap(lax.dynamic_slice_in_dim(rows_w, (1 - my_head) * half, half, 1), "head")

    def slab(w, s):
        return lax.dynamic_slice_in_dim(w, s * width, width, 0)

    weights = jnp.concatenate(
        [slab(keep_w, my_seq), slab(other_w, my_seq), slab(keep_w, 1 - my_seq), slab(other_w, 1 - my_seq)], 0
    )

    recv, assign, segs, scaled, weights = lax.optimization_barrier((recv, assign, segs, scaled, weights))

    row_at = jnp.asarray(ROW_AT, jnp.int32)[me]
    place_of = jnp.asarray(PLACE_OF, jnp.int32)[me]
    attend = functools.partial(
        attend_rows, assign=assign, row_at=row_at, place_of=place_of, segs=segs, labels=advantage.shape[1], heads=mine
    )
    across, middle = ((0, 1), (1, 0), (2, 3), (3, 2)), ((1, 2), (2, 1))

    def send(x, perm, name):
        with jax.named_scope(name):
            return lax.ppermute(x, "dp", perm)

    inner = (me == 1) | (me == 2)

    from_2, mid_1 = send(scaled, across, "swap_0"), send(scaled, middle, "mid_0")

    far = attend((0, 1), recv)
    far_seq, far_head = swap(far, "seq", "far_seq"), swap(far, "head", "far_head")
    near = attend((2, 3), recv)
    far_seq, near = lax.optimization_barrier((far_seq, near))
    far_diag = swap(far_seq, "head", "far_diag")
    near_seq, near_head = swap(near, "seq", "near_seq"), swap(near, "head", "near_head")
    first, second = project((far, far_head, far_seq, far_diag), weights)
    near_diag = swap(near_seq, "head", "near_diag")
    third, own = project((near, near_head, near_seq, near_diag), weights)

    first, from_2 = lax.optimization_barrier((first, from_2))
    swapped_1 = send(jnp.where(inner, mid_1, first), across, "swap_1")
    mid_0 = send(from_2, middle, "mid_1")
    swapped_1, mid_0, second, third = lax.optimization_barrier((swapped_1, mid_0, second, third))
    swapped_2 = send(jnp.where(inner, mid_0, second), across, "swap_2")
    crossed_2 = send(add(first, swapped_1), middle, "mid_2")
    swapped_2, crossed_2 = lax.optimization_barrier((swapped_2, crossed_2))
    to_swap, second = lax.optimization_barrier((add(third, crossed_2), second))
    swapped_3 = send(to_swap, across, "swap_3")
    crossed_3 = send(add(second, swapped_2), middle, "mid_3")

    pieces = [jnp.where(inner, mid_0, swapped_2), jnp.where(inner, mid_1, swapped_1), from_2, scaled]
    others = [swap(x, "head", f"piece_{i}") for i, x in enumerate(pieces)]
    grad = weight_gradient((far, near), (far_seq, near_seq), pieces, others, my_seq, my_head)
    swapped_3, crossed_3, grad = lax.optimization_barrier((swapped_3, crossed_3, grad))
    mixed = own.astype(jnp.float32) + swapped_3.astype(jnp.float32) + crossed_3.astype(jnp.float32)
    return mixed.astype(jnp.bfloat16), grad.reshape(nseq * mine, 1, head_size, cols)


def solution(mesh):
    placed = (
        P(None, ("groups", "dp", "seq"), None, "head", None),
        P(("groups", "dp"), "seq", None),
        P(("groups", "dp"), None),
        P(("groups", "dp"), None),
        P("dp", "head", None, "seq"),
        P(("groups", "dp"), "seq"),
    )

    def body(projected, *rest):
        ndp, nseq = mesh.shape["dp"], mesh.shape["seq"]
        fits = projected.shape[2] % (ndp * nseq) == 0 and (ndp, nseq) == (4, 2)
        return (body_heads if fits else body_rows)(projected, *rest)

    return jax.shard_map(
        body,
        mesh=mesh,
        in_specs=placed,
        out_specs=(P(("groups", "dp"), ("seq", "head")), P(("groups", "dp"), "head", None, "seq")),
        check_vma=False,
    )
```

```python
import functools
import math

import jax
import jax.numpy as jnp
from jax import lax
from jax.experimental import pallas as pl
from jax.experimental.pallas import tpu as pltpu
from jax.sharding import PartitionSpec as P

CAP = 2
SHORT = pl.CostEstimate(flops=1000, bytes_accessed=1000, transcendentals=0)
ROW_AT = ((3, 2, 1, 0), (3, 2, 0, 1), (0, 1, 3, 2), (0, 1, 2, 3))
PLACE_OF = ((3, 2, 1, 0), (2, 3, 1, 0), (0, 1, 3, 2), (0, 1, 2, 3))


def attend_heads(queries, keys_all, values_all, seg_query, seg_key):
    head_size = queries.shape[-1]
    scores = jnp.einsum("tkc,ukc->ktu", queries, keys_all, preferred_element_type=jnp.float32) * (
        1.0 / math.sqrt(head_size)
    )
    pos_query = jnp.arange(queries.shape[0], dtype=jnp.int32)
    pos_key = jnp.arange(keys_all.shape[0], dtype=jnp.int32)
    keep = (seg_query[:, None] == seg_key[None, :]) & (pos_key[None, :] <= pos_query[:, None])
    scores = jnp.where(keep[None], scores, -1e30)
    rowmax = jnp.max(scores, axis=-1, keepdims=True)
    expd = jnp.where(keep[None], jnp.exp(scores - rowmax), 0.0)
    probs = (expd / jnp.sum(expd, axis=-1, keepdims=True)).astype(jnp.bfloat16)
    attended = jnp.einsum("ktu,ukc->tkc", probs, values_all, preferred_element_type=jnp.float32)
    return attended.astype(jnp.bfloat16)


def token_weight(seg_row, adv_row):
    labels = jnp.arange(adv_row.shape[0], dtype=jnp.int32)
    member_seg = (seg_row[:, None] == labels[None, :]).astype(jnp.float32)
    sizes_tok = jnp.sum(member_seg * jnp.sum(member_seg, axis=0)[None, :], axis=1)
    adv_tok = jnp.sum(member_seg * adv_row[None, :], axis=1)
    return adv_tok / sizes_tok


def body_rows(projected, assignment, segments, advantage, out_weight, cotangent):
    shards = lax.axis_size("dp")
    tok_rows = projected.shape[1]
    head_count = projected.shape[2]
    head_size = projected.shape[4]
    block_len = tok_rows // shards
    out_cols = out_weight.shape[3]
    blocks = jnp.transpose(
        projected.reshape(3, shards, block_len, head_count, head_size), (1, 0, 2, 3, 4)
    )
    targets = assignment.reshape(shards)
    member = (targets[:, None] == jnp.arange(shards, dtype=jnp.int32)[None, :]).astype(jnp.int32)
    ranks = jnp.sum((jnp.cumsum(member, axis=0) - member) * member, axis=1)
    counts = jnp.sum(member, axis=0).reshape(shards, 1)
    outgoing = jnp.zeros((shards, CAP, 3, block_len, head_count, head_size), projected.dtype)
    outgoing = outgoing.at[targets, ranks].set(blocks)
    incoming, arrived = (
        lax.all_to_all(outgoing, "dp", split_axis=0, concat_axis=0, tiled=True),
        lax.all_to_all(counts, "dp", split_axis=0, concat_axis=0, tiled=True),
    )
    arrived = arrived.reshape(shards)
    firsts = jnp.cumsum(arrived) - arrived
    slots = jnp.arange(CAP, dtype=jnp.int32)
    places = jnp.where(slots[None, :] < arrived[:, None], firsts[:, None] + slots[None, :], shards)
    packed = jnp.zeros((shards, 3, block_len, head_count, head_size), projected.dtype)
    packed = packed.at[places.reshape(-1)].set(
        incoming.reshape(shards * CAP, 3, block_len, head_count, head_size), mode="drop"
    )
    local = jnp.transpose(packed, (1, 0, 2, 3, 4)).reshape(3, tok_rows, head_count, head_size)
    seg_row = segments[0]
    weight = token_weight(seg_row, advantage[0])
    scaled = (cotangent.astype(jnp.float32) * weight[:, None]).astype(jnp.bfloat16)
    gathered = lax.all_gather(out_weight, "dp", axis=0, tiled=True)
    weight_rows = gathered.reshape(head_count, head_size, out_cols)
    switched = lax.all_to_all(local, "seq", split_axis=2, concat_axis=1, tiled=True)
    attended = attend_heads(switched[0], switched[1], switched[2], seg_row, seg_row)
    piece = lax.all_gather(attended, "seq", axis=1, tiled=True)
    total = jnp.einsum("tkc,kcn->tn", piece, weight_rows, preferred_element_type=jnp.float32)
    term = jnp.einsum("tkc,tn->kcn", piece, scaled, preferred_element_type=jnp.float32)
    mixed = lax.psum_scatter(total.astype(jnp.bfloat16), "head", scatter_dimension=1, tiled=True)
    weight_grad = lax.psum_scatter(
        term.reshape(head_count, 1, head_size, out_cols).astype(jnp.bfloat16),
        "dp",
        scatter_dimension=0,
        tiled=True,
    ).astype(jnp.float32)
    return (mixed, weight_grad)


def pack_kernel(assign, segs, x, out):
    peers, rows, head_size = out.shape
    _, tokens, pairs, _ = x.shape
    mine = pairs // peers
    row_len = segs.shape[1]
    line = lax.broadcasted_iota(jnp.int32, (16, head_size), 0)
    lane = lax.broadcasted_iota(jnp.int32, (16, head_size), 1)
    small = jnp.zeros((16, head_size), jnp.int32)
    for i in range(row_len // head_size):
        small = jnp.where(line == i, segs[:, i * head_size : (i + 1) * head_size], small)
    for i in range(assign.shape[1]):
        small = jnp.where((line == row_len // head_size) & (lane == i), assign[:, i : i + 1], small)
    small = small.astype(jnp.float32).astype(jnp.bfloat16)
    for p in range(peers):
        out[p, rows - 16 :, :] = small
    for c in range(3):
        turned = jnp.swapaxes(x[c], 0, 1)
        for p in range(peers):
            for i in range(mine):
                first = (c * mine + i) * tokens
                out[p, first : first + tokens, :] = turned[p * mine + i]


def pack(x, segs, assign, peers):
    _, tokens, pairs, head_size = x.shape
    vmem = pl.BlockSpec(memory_space=pltpu.VMEM)
    return pl.pallas_call(
        pack_kernel,
        out_shape=jax.ShapeDtypeStruct((peers, 3 * tokens * pairs // peers + 16, head_size), x.dtype),
        in_specs=[vmem, vmem, vmem],
        out_specs=vmem,
        compiler_params=pltpu.CompilerParams(vmem_limit_bytes=60 << 20),
        cost_estimate=SHORT,
        name="pack",
    )(assign, segs, x)


def attention_kernel(places, labels, nblk, blk, assign, row_at, place_of, segs, recv, out, packed, order):
    heads, row_len, head_size = packed.shape[1:]
    tokens = nblk * blk
    rows = segs.shape[0]
    nseq = recv.shape[0] // rows
    per_shard = row_len // nseq // blk
    for s in range(nseq):
        counts = [jnp.int32(0)] * rows
        for o in range(rows):
            for b in range(nblk):
                target = place_of[assign[o * nseq + s, b]]
                slot = counts[0]
                for r in range(1, rows):
                    slot = jnp.where(target == r, counts[r], slot)
                order[(target * nseq + s) * per_shard + slot] = o * nblk + b
                counts = [counts[r] + (target == r).astype(jnp.int32) for r in range(rows)]
    pos_query = lax.broadcasted_iota(jnp.int32, (row_len, 1), 0)
    pos_key = lax.broadcasted_iota(jnp.int32, (1, row_len), 1)
    causal = pos_key <= pos_query
    scale = 1.0 / math.sqrt(head_size)
    for i, r in enumerate(places):
        ids = segs[pl.ds(row_at[r], 1), :]
        query_id, key_id = jnp.zeros_like(pos_query), ids
        for label in range(1, labels):
            lower = jnp.sum((ids < label).astype(jnp.int32), axis=1, keepdims=True)
            query_id = query_id + (pos_query >= lower).astype(jnp.int32)
        keep = causal & (query_id == key_id)
        for s in range(nseq):
            for slot in range(per_shard):
                source = order[(r * nseq + s) * per_shard + slot]
                owner, block = lax.div(source, nblk), lax.rem(source, nblk)
                first = pl.multiple_of(block * blk, blk)
                place = (s * per_shard + slot) * blk
                for c in range(3):
                    for h in range(heads):
                        packed[c, h, place : place + blk, :] = recv[
                            owner * nseq + s, pl.ds((c * heads + h) * tokens + first, blk), :
                        ]
        for h in range(heads):
            scores = lax.dot_general(
                packed[0, h], packed[1, h], (((1,), (1,)), ((), ())), preferred_element_type=jnp.float32
            ) * scale
            scores = jnp.where(keep, scores, -1e30)
            rowmax = jnp.max(scores, axis=-1, keepdims=True)
            expd = jnp.where(keep, jnp.exp(scores - rowmax), 0.0)
            probs = (expd / jnp.sum(expd, axis=-1, keepdims=True)).astype(jnp.bfloat16)
            attended = jnp.dot(probs, packed[2, h], preferred_element_type=jnp.float32)
            out[i * row_len : (i + 1) * row_len, h * head_size : (h + 1) * head_size] = attended.astype(
                jnp.bfloat16
            )


def attend_rows(places, recv, assign, row_at, place_of, segs, labels, heads):
    head_size = recv.shape[2]
    rows, row_len = segs.shape
    nblk = assign.shape[1]
    tokens = row_len * rows // recv.shape[0]
    count = len(places)
    smem, vmem = pl.BlockSpec(memory_space=pltpu.SMEM), pl.BlockSpec(memory_space=pltpu.VMEM)
    return pl.pallas_call(
        functools.partial(attention_kernel, places, labels, nblk, tokens // nblk),
        out_shape=jax.ShapeDtypeStruct((count * row_len, heads * head_size), jnp.bfloat16),
        in_specs=[smem, smem, smem, vmem, vmem],
        out_specs=vmem,
        scratch_shapes=[
            pltpu.VMEM((3, heads, row_len, head_size), jnp.bfloat16),
            pltpu.SMEM((recv.shape[0] * nblk,), jnp.int32),
        ],
        compiler_params=pltpu.CompilerParams(vmem_limit_bytes=10 << 20),
        cost_estimate=SHORT,
        name="attend_rows",
    )(assign, row_at, place_of, segs, recv)


def project_kernel(tile, *refs):
    parts, weights, outs = refs[:-3], refs[-3], refs[-2:]
    rows = jnp.concatenate([x[...] for x in parts], 1)

    @pl.loop(0, weights.shape[1] // tile)
    def _(t):
        columns = pl.ds(pl.multiple_of(t * tile, tile), tile)
        total = jnp.dot(rows, weights[:, columns], preferred_element_type=jnp.float32).astype(jnp.bfloat16)
        for i, out in enumerate(outs):
            out[:, columns] = total[i * out.shape[0] : (i + 1) * out.shape[0]]


def project(parts, weights):
    tokens = parts[0].shape[0]
    half = weights.shape[1]
    vmem = pl.BlockSpec(memory_space=pltpu.VMEM)
    return pl.pallas_call(
        functools.partial(project_kernel, math.gcd(half, 256)),
        out_shape=[jax.ShapeDtypeStruct((tokens // 2, half), jnp.bfloat16)] * 2,
        in_specs=[vmem] * (len(parts) + 1),
        out_specs=[vmem] * 2,
        compiler_params=pltpu.CompilerParams(vmem_limit_bytes=14 << 20),
        cost_estimate=SHORT,
        name="project",
    )(*parts, weights)


def gradient_kernel(place, far, near, far_seq, near_seq, *refs):
    own, other, out, turned = refs[:4], refs[4:8], refs[8], refs[9]
    width = far.shape[1]
    row_len = own[0].shape[0]

    @pl.when((pl.program_id(0) == 0) & (pl.program_id(1) == 0))
    def _():
        for s, parts in enumerate(((far, near), (far_seq, near_seq))):
            first = pl.multiple_of(width * (place[0] if s == 0 else 1 - place[0]), width)
            for i, part in enumerate(parts):
                turned[pl.ds(first, width), 2 * i * row_len : 2 * (i + 1) * row_len] = part[...].T

    for side, group in enumerate((own, other)):

        @pl.when(pl.program_id(0) == side)
        def _():
            rows = jnp.concatenate([x[...] for x in group], 0)
            out[...] = jnp.dot(turned[...], rows, preferred_element_type=jnp.float32)


def weight_gradient(att, att_seq, pieces, others, my_seq, my_head):
    width = att[0].shape[1]
    row_len, half = pieces[0].shape
    tile = math.gcd(half, 640)
    tiles = half // tile
    whole = pl.BlockSpec(att[0].shape, lambda side, t, place: (0, 0))
    own = pl.BlockSpec((row_len, tile), lambda side, t, place: (0, jnp.where(side == 0, t, tiles - 1)))
    other = pl.BlockSpec((row_len, tile), lambda side, t, place: (0, jnp.where(side == 0, 0, t)))
    out = pl.BlockSpec(
        (2 * width, tile), lambda side, t, place: (0, jnp.where(side == 0, place[1], 1 - place[1]) * tiles + t)
    )
    return pl.pallas_call(
        gradient_kernel,
        out_shape=jax.ShapeDtypeStruct((2 * width, 2 * half), jnp.float32),
        grid_spec=pltpu.PrefetchScalarGridSpec(
            num_scalar_prefetch=1,
            grid=(2, tiles),
            in_specs=[whole] * 4 + [own] * 4 + [other] * 4,
            out_specs=out,
            scratch_shapes=[pltpu.VMEM((2 * width, 4 * row_len), jnp.bfloat16)],
        ),
        compiler_params=pltpu.CompilerParams(vmem_limit_bytes=20 << 20),
        cost_estimate=SHORT,
        name="weight_gradient",
    )(jnp.stack([my_seq, my_head]).astype(jnp.int32), *att, *att_seq, *pieces, *others)


def swap(x, axis, name="swap"):
    with jax.named_scope(name):
        return lax.ppermute(x, axis, [(0, 1), (1, 0)])


def add(x, y):
    return (x.astype(jnp.float32) + y.astype(jnp.float32)).astype(jnp.bfloat16)


def body_heads(projected, assignment, segments, advantage, out_weight, cotangent):
    ndp, nseq = lax.axis_size("dp"), lax.axis_size("seq")
    me, my_seq, my_head = lax.axis_index("dp"), lax.axis_index("seq"), lax.axis_index("head")
    tokens, pairs, head_size = projected.shape[1], projected.shape[2], projected.shape[4]
    nblk = assignment.shape[2]
    row_len = segments.shape[1]
    peers = ndp * nseq
    mine = pairs // peers
    cols = out_weight.shape[3]
    half = cols // 2
    width = mine * head_size

    sent = pack(projected.reshape(3, tokens, pairs, head_size), segments, assignment.reshape(1, nblk), peers)
    recv = lax.all_to_all(sent, ("dp", "seq"), split_axis=0, concat_axis=0, tiled=True)
    small = recv[:, 3 * mine * tokens :].astype(jnp.int32).reshape(peers, 16 * head_size)
    assign, segs = small[:, row_len : row_len + nblk], small[::nseq, :row_len]

    weight = token_weight(segments[0], advantage[0])
    own_cols = lax.dynamic_slice_in_dim(cotangent, my_head * half, half, 1)
    scaled = (own_cols.astype(jnp.float32) * weight[:, None]).astype(jnp.bfloat16)

    rows_w = out_weight.reshape(nseq * width, cols)
    keep_w = lax.dynamic_slice_in_dim(rows_w, my_head * half, half, 1)
    other_w = swap(lax.dynamic_slice_in_dim(rows_w, (1 - my_head) * half, half, 1), "head")

    def slab(w, s):
        return lax.dynamic_slice_in_dim(w, s * width, width, 0)

    weights = jnp.concatenate(
        [slab(keep_w, my_seq), slab(other_w, my_seq), slab(keep_w, 1 - my_seq), slab(other_w, 1 - my_seq)], 0
    )

    row_at = jnp.asarray(ROW_AT, jnp.int32)[me]
    place_of = jnp.asarray(PLACE_OF, jnp.int32)[me]
    early = scaled
    recv, assign, segs, scaled, weights, row_at, place_of = lax.optimization_barrier(
        (recv, assign, segs, scaled, weights, row_at, place_of)
    )

    attend = functools.partial(
        attend_rows, assign=assign, row_at=row_at, place_of=place_of, segs=segs, labels=advantage.shape[1], heads=mine
    )
    across, middle = ((0, 1), (1, 0), (2, 3), (3, 2)), ((1, 2), (2, 1))

    def send(x, perm, name):
        with jax.named_scope(name):
            return lax.ppermute(x, "dp", perm)

    inner = (me == 1) | (me == 2)

    from_2, mid_1 = send(early, across, "swap_0"), send(scaled, middle, "mid_0")

    far = attend((0, 1), recv)
    far, from_2 = lax.optimization_barrier((far, from_2))
    far_seq, far_head = swap(far, "seq", "far_seq"), swap(far, "head", "far_head")
    near = attend((2, 3), recv)
    far_seq, near = lax.optimization_barrier((far_seq, near))
    far_diag = swap(far_seq, "head", "far_diag")
    near_seq, near_head = swap(near, "seq", "near_seq"), swap(near, "head", "near_head")
    first, second = project((far, far_head, far_seq, far_diag), weights)
    near_diag = swap(near_seq, "head", "near_diag")
    third, own = project((near, near_head, near_seq, near_diag), weights)

    to_swap, from_2 = lax.optimization_barrier((jnp.where(inner, mid_1, first), from_2))
    swapped_1 = send(to_swap, across, "swap_1")
    mid_0 = send(from_2, middle, "mid_1")
    swapped_1, mid_0, second, third = lax.optimization_barrier((swapped_1, mid_0, second, third))
    swapped_2 = send(jnp.where(inner, mid_0, second), across, "swap_2")
    crossed_2 = send(add(first, swapped_1), middle, "mid_2")
    swapped_2, crossed_2 = lax.optimization_barrier((swapped_2, crossed_2))
    to_swap, second = lax.optimization_barrier((add(third, crossed_2), second))
    swapped_3 = send(to_swap, across, "swap_3")
    crossed_3 = send(add(second, swapped_2), middle, "mid_3")

    pieces = [jnp.where(inner, mid_0, swapped_2), jnp.where(inner, mid_1, swapped_1), from_2, scaled]
    others = [swap(x, "head", f"piece_{i}") for i, x in enumerate(pieces)]
    grad = weight_gradient((far, near), (far_seq, near_seq), pieces, others, my_seq, my_head)
    swapped_3, grad = lax.optimization_barrier((swapped_3, grad))
    mixed = own.astype(jnp.float32) + swapped_3.astype(jnp.float32) + crossed_3.astype(jnp.float32)
    return mixed.astype(jnp.bfloat16), grad.reshape(nseq * mine, 1, head_size, cols)


def solution(mesh):
    placed = (
        P(None, ("groups", "dp", "seq"), None, "head", None),
        P(("groups", "dp"), "seq", None),
        P(("groups", "dp"), None),
        P(("groups", "dp"), None),
        P("dp", "head", None, "seq"),
        P(("groups", "dp"), "seq"),
    )

    def body(projected, *rest):
        ndp, nseq = mesh.shape["dp"], mesh.shape["seq"]
        fits = projected.shape[2] % (ndp * nseq) == 0 and (ndp, nseq) == (4, 2)
        return (body_heads if fits else body_rows)(projected, *rest)

    return jax.shard_map(
        body,
        mesh=mesh,
        in_specs=placed,
        out_specs=(P(("groups", "dp"), ("seq", "head")), P(("groups", "dp"), "head", None, "seq")),
        check_vma=False,
    )
```

```python
import functools
import math

import jax
import jax.numpy as jnp
from jax import lax
from jax.experimental import pallas as pl
from jax.experimental.pallas import tpu as pltpu
from jax.sharding import PartitionSpec as P

CAP = 2
SHORT = pl.CostEstimate(flops=1000, bytes_accessed=1000, transcendentals=0)
ROW_AT = ((3, 2, 1, 0), (3, 2, 0, 1), (0, 1, 3, 2), (0, 1, 2, 3))
PLACE_OF = ((3, 2, 1, 0), (2, 3, 1, 0), (0, 1, 3, 2), (0, 1, 2, 3))


def attend_heads(queries, keys_all, values_all, seg_query, seg_key):
    head_size = queries.shape[-1]
    scores = jnp.einsum("tkc,ukc->ktu", queries, keys_all, preferred_element_type=jnp.float32) * (
        1.0 / math.sqrt(head_size)
    )
    pos_query = jnp.arange(queries.shape[0], dtype=jnp.int32)
    pos_key = jnp.arange(keys_all.shape[0], dtype=jnp.int32)
    keep = (seg_query[:, None] == seg_key[None, :]) & (pos_key[None, :] <= pos_query[:, None])
    scores = jnp.where(keep[None], scores, -1e30)
    rowmax = jnp.max(scores, axis=-1, keepdims=True)
    expd = jnp.where(keep[None], jnp.exp(scores - rowmax), 0.0)
    probs = (expd / jnp.sum(expd, axis=-1, keepdims=True)).astype(jnp.bfloat16)
    attended = jnp.einsum("ktu,ukc->tkc", probs, values_all, preferred_element_type=jnp.float32)
    return attended.astype(jnp.bfloat16)


def token_weight(seg_row, adv_row):
    labels = jnp.arange(adv_row.shape[0], dtype=jnp.int32)
    member_seg = (seg_row[:, None] == labels[None, :]).astype(jnp.float32)
    sizes_tok = jnp.sum(member_seg * jnp.sum(member_seg, axis=0)[None, :], axis=1)
    adv_tok = jnp.sum(member_seg * adv_row[None, :], axis=1)
    return adv_tok / sizes_tok


def body_rows(projected, assignment, segments, advantage, out_weight, cotangent):
    shards = lax.axis_size("dp")
    tok_rows = projected.shape[1]
    head_count = projected.shape[2]
    head_size = projected.shape[4]
    block_len = tok_rows // shards
    out_cols = out_weight.shape[3]
    blocks = jnp.transpose(
        projected.reshape(3, shards, block_len, head_count, head_size), (1, 0, 2, 3, 4)
    )
    targets = assignment.reshape(shards)
    member = (targets[:, None] == jnp.arange(shards, dtype=jnp.int32)[None, :]).astype(jnp.int32)
    ranks = jnp.sum((jnp.cumsum(member, axis=0) - member) * member, axis=1)
    counts = jnp.sum(member, axis=0).reshape(shards, 1)
    outgoing = jnp.zeros((shards, CAP, 3, block_len, head_count, head_size), projected.dtype)
    outgoing = outgoing.at[targets, ranks].set(blocks)
    incoming, arrived = (
        lax.all_to_all(outgoing, "dp", split_axis=0, concat_axis=0, tiled=True),
        lax.all_to_all(counts, "dp", split_axis=0, concat_axis=0, tiled=True),
    )
    arrived = arrived.reshape(shards)
    firsts = jnp.cumsum(arrived) - arrived
    slots = jnp.arange(CAP, dtype=jnp.int32)
    places = jnp.where(slots[None, :] < arrived[:, None], firsts[:, None] + slots[None, :], shards)
    packed = jnp.zeros((shards, 3, block_len, head_count, head_size), projected.dtype)
    packed = packed.at[places.reshape(-1)].set(
        incoming.reshape(shards * CAP, 3, block_len, head_count, head_size), mode="drop"
    )
    local = jnp.transpose(packed, (1, 0, 2, 3, 4)).reshape(3, tok_rows, head_count, head_size)
    seg_row = segments[0]
    weight = token_weight(seg_row, advantage[0])
    scaled = (cotangent.astype(jnp.float32) * weight[:, None]).astype(jnp.bfloat16)
    gathered = lax.all_gather(out_weight, "dp", axis=0, tiled=True)
    weight_rows = gathered.reshape(head_count, head_size, out_cols)
    switched = lax.all_to_all(local, "seq", split_axis=2, concat_axis=1, tiled=True)
    attended = attend_heads(switched[0], switched[1], switched[2], seg_row, seg_row)
    piece = lax.all_gather(attended, "seq", axis=1, tiled=True)
    total = jnp.einsum("tkc,kcn->tn", piece, weight_rows, preferred_element_type=jnp.float32)
    term = jnp.einsum("tkc,tn->kcn", piece, scaled, preferred_element_type=jnp.float32)
    mixed = lax.psum_scatter(total.astype(jnp.bfloat16), "head", scatter_dimension=1, tiled=True)
    weight_grad = lax.psum_scatter(
        term.reshape(head_count, 1, head_size, out_cols).astype(jnp.bfloat16),
        "dp",
        scatter_dimension=0,
        tiled=True,
    ).astype(jnp.float32)
    return (mixed, weight_grad)


def pack_kernel(assign, segs, x, out):
    peers, rows, head_size = out.shape
    _, tokens, pairs, _ = x.shape
    mine = pairs // peers
    row_len = segs.shape[1]
    line = lax.broadcasted_iota(jnp.int32, (16, head_size), 0)
    lane = lax.broadcasted_iota(jnp.int32, (16, head_size), 1)
    small = jnp.zeros((16, head_size), jnp.int32)
    for i in range(row_len // head_size):
        small = jnp.where(line == i, segs[:, i * head_size : (i + 1) * head_size], small)
    for i in range(assign.shape[1]):
        small = jnp.where((line == row_len // head_size) & (lane == i), assign[:, i : i + 1], small)
    small = small.astype(jnp.float32).astype(jnp.bfloat16)
    for p in range(peers):
        out[p, rows - 16 :, :] = small
    for c in range(3):
        turned = jnp.swapaxes(x[c], 0, 1)
        for p in range(peers):
            for i in range(mine):
                first = (c * mine + i) * tokens
                out[p, first : first + tokens, :] = turned[p * mine + i]


def pack(x, segs, assign, peers):
    _, tokens, pairs, head_size = x.shape
    vmem = pl.BlockSpec(memory_space=pltpu.VMEM)
    return pl.pallas_call(
        pack_kernel,
        out_shape=jax.ShapeDtypeStruct((peers, 3 * tokens * pairs // peers + 16, head_size), x.dtype),
        in_specs=[vmem, vmem, vmem],
        out_specs=vmem,
        compiler_params=pltpu.CompilerParams(vmem_limit_bytes=60 << 20),
        cost_estimate=SHORT,
        name="pack",
    )(assign, segs, x)


def attention_kernel(places, labels, nblk, blk, assign, row_at, place_of, segs, recv, out, packed, order):
    heads, row_len, head_size = packed.shape[1:]
    tokens = nblk * blk
    rows = segs.shape[0]
    nseq = recv.shape[0] // rows
    per_shard = row_len // nseq // blk
    for s in range(nseq):
        counts = [jnp.int32(0)] * rows
        for o in range(rows):
            for b in range(nblk):
                target = place_of[assign[o * nseq + s, b]]
                slot = counts[0]
                for r in range(1, rows):
                    slot = jnp.where(target == r, counts[r], slot)
                order[(target * nseq + s) * per_shard + slot] = o * nblk + b
                counts = [counts[r] + (target == r).astype(jnp.int32) for r in range(rows)]
    pos_query = lax.broadcasted_iota(jnp.int32, (row_len, 1), 0)
    pos_key = lax.broadcasted_iota(jnp.int32, (1, row_len), 1)
    causal = pos_key <= pos_query
    scale = 1.0 / math.sqrt(head_size)
    for i, r in enumerate(places):
        ids = segs[pl.ds(row_at[r], 1), :]
        query_id, key_id = jnp.zeros_like(pos_query), ids
        for label in range(1, labels):
            lower = jnp.sum((ids < label).astype(jnp.int32), axis=1, keepdims=True)
            query_id = query_id + (pos_query >= lower).astype(jnp.int32)
        keep = causal & (query_id == key_id)
        for s in range(nseq):
            for slot in range(per_shard):
                source = order[(r * nseq + s) * per_shard + slot]
                owner, block = lax.div(source, nblk), lax.rem(source, nblk)
                first = pl.multiple_of(block * blk, blk)
                place = (s * per_shard + slot) * blk
                for c in range(3):
                    for h in range(heads):
                        packed[c, h, place : place + blk, :] = recv[
                            owner * nseq + s, pl.ds((c * heads + h) * tokens + first, blk), :
                        ]
        for h in range(heads):
            scores = lax.dot_general(
                packed[0, h], packed[1, h], (((1,), (1,)), ((), ())), preferred_element_type=jnp.float32
            ) * scale
            scores = jnp.where(keep, scores, -1e30)
            rowmax = jnp.max(scores, axis=-1, keepdims=True)
            expd = jnp.where(keep, jnp.exp(scores - rowmax), 0.0)
            probs = (expd / jnp.sum(expd, axis=-1, keepdims=True)).astype(jnp.bfloat16)
            attended = jnp.dot(probs, packed[2, h], preferred_element_type=jnp.float32)
            out[i * row_len : (i + 1) * row_len, h * head_size : (h + 1) * head_size] = attended.astype(
                jnp.bfloat16
            )


def attend_rows(places, recv, assign, row_at, place_of, segs, labels, heads):
    head_size = recv.shape[2]
    rows, row_len = segs.shape
    nblk = assign.shape[1]
    tokens = row_len * rows // recv.shape[0]
    count = len(places)
    smem, vmem = pl.BlockSpec(memory_space=pltpu.SMEM), pl.BlockSpec(memory_space=pltpu.VMEM)
    return pl.pallas_call(
        functools.partial(attention_kernel, places, labels, nblk, tokens // nblk),
        out_shape=jax.ShapeDtypeStruct((count * row_len, heads * head_size), jnp.bfloat16),
        in_specs=[smem, smem, smem, vmem, vmem],
        out_specs=vmem,
        scratch_shapes=[
            pltpu.VMEM((3, heads, row_len, head_size), jnp.bfloat16),
            pltpu.SMEM((recv.shape[0] * nblk,), jnp.int32),
        ],
        compiler_params=pltpu.CompilerParams(vmem_limit_bytes=10 << 20),
        cost_estimate=SHORT,
        name="attend_rows",
    )(assign, row_at, place_of, segs, recv)


def project_kernel(tile, *refs):
    parts, weights, outs = refs[:4], refs[4], refs[5:]
    rows = jnp.concatenate([x[...] for x in parts], 1)

    @pl.loop(0, weights.shape[1] // tile)
    def _(t):
        columns = pl.ds(pl.multiple_of(t * tile, tile), tile)
        total = jnp.dot(rows, weights[:, columns], preferred_element_type=jnp.float32).astype(jnp.bfloat16)
        for i, out in enumerate(outs):
            out[:, columns] = total[i * out.shape[0] : (i + 1) * out.shape[0]]


def project(parts, weights, row_len):
    count = parts[0].shape[0] // row_len
    half = weights.shape[1]
    vmem = pl.BlockSpec(memory_space=pltpu.VMEM)
    return pl.pallas_call(
        functools.partial(project_kernel, math.gcd(half, 256)),
        out_shape=[jax.ShapeDtypeStruct((row_len, half), jnp.bfloat16)] * count,
        in_specs=[vmem] * (len(parts) + 1),
        out_specs=[vmem] * count,
        compiler_params=pltpu.CompilerParams(vmem_limit_bytes=14 << 20),
        cost_estimate=SHORT,
        name="project",
    )(*parts, weights)


def gradient_kernel(place, far, near, far_seq, near_seq, *refs):
    own, other, out, turned = refs[:4], refs[4:8], refs[8], refs[9]
    width = far.shape[1]
    row_len = own[0].shape[0]

    @pl.when((pl.program_id(0) == 0) & (pl.program_id(1) == 0))
    def _():
        for s, parts in enumerate(((far, near), (far_seq, near_seq))):
            first = pl.multiple_of(width * (place[0] if s == 0 else 1 - place[0]), width)
            done = 0
            for part in parts:
                turned[pl.ds(first, width), done : done + part.shape[0]] = part[...].T
                done += part.shape[0]

    for side, group in enumerate((own, other)):

        @pl.when(pl.program_id(0) == side)
        def _():
            rows = jnp.concatenate([x[...] for x in group], 0)
            out[...] = jnp.dot(turned[...], rows, preferred_element_type=jnp.float32)


def weight_gradient(att, att_seq, pieces, others, my_seq, my_head):
    width = att[0].shape[1]
    row_len, half = pieces[0].shape
    tile = math.gcd(half, 640)
    tiles = half // tile
    whole = [pl.BlockSpec(x.shape, lambda side, t, place: (0, 0)) for x in (*att, *att_seq)]
    own = pl.BlockSpec((row_len, tile), lambda side, t, place: (0, jnp.where(side == 0, t, tiles - 1)))
    other = pl.BlockSpec((row_len, tile), lambda side, t, place: (0, jnp.where(side == 0, 0, t)))
    out = pl.BlockSpec(
        (2 * width, tile), lambda side, t, place: (0, jnp.where(side == 0, place[1], 1 - place[1]) * tiles + t)
    )
    return pl.pallas_call(
        gradient_kernel,
        out_shape=jax.ShapeDtypeStruct((2 * width, 2 * half), jnp.float32),
        grid_spec=pltpu.PrefetchScalarGridSpec(
            num_scalar_prefetch=1,
            grid=(2, tiles),
            in_specs=whole + [own] * 4 + [other] * 4,
            out_specs=out,
            scratch_shapes=[pltpu.VMEM((2 * width, 4 * row_len), jnp.bfloat16)],
        ),
        compiler_params=pltpu.CompilerParams(vmem_limit_bytes=20 << 20),
        cost_estimate=SHORT,
        name="weight_gradient",
    )(jnp.stack([my_seq, my_head]).astype(jnp.int32), *att, *att_seq, *pieces, *others)


def swap(x, axis, name="swap"):
    with jax.named_scope(name):
        return lax.ppermute(x, axis, [(0, 1), (1, 0)])


def add(x, y):
    return (x.astype(jnp.float32) + y.astype(jnp.float32)).astype(jnp.bfloat16)


def body_heads(projected, assignment, segments, advantage, out_weight, cotangent):
    ndp, nseq = lax.axis_size("dp"), lax.axis_size("seq")
    me, my_seq, my_head = lax.axis_index("dp"), lax.axis_index("seq"), lax.axis_index("head")
    tokens, pairs, head_size = projected.shape[1], projected.shape[2], projected.shape[4]
    nblk = assignment.shape[2]
    row_len = segments.shape[1]
    peers = ndp * nseq
    mine = pairs // peers
    cols = out_weight.shape[3]
    half = cols // 2
    width = mine * head_size

    sent = pack(projected.reshape(3, tokens, pairs, head_size), segments, assignment.reshape(1, nblk), peers)
    recv = lax.all_to_all(sent, ("dp", "seq"), split_axis=0, concat_axis=0, tiled=True)
    small = recv[:, 3 * mine * tokens :].astype(jnp.int32).reshape(peers, 16 * head_size)
    assign, segs = small[:, row_len : row_len + nblk], small[::nseq, :row_len]

    weight = token_weight(segments[0], advantage[0])
    own_cols = lax.dynamic_slice_in_dim(cotangent, my_head * half, half, 1)
    scaled = (own_cols.astype(jnp.float32) * weight[:, None]).astype(jnp.bfloat16)

    rows_w = out_weight.reshape(nseq * width, cols)
    keep_w = lax.dynamic_slice_in_dim(rows_w, my_head * half, half, 1)
    other_w = swap(lax.dynamic_slice_in_dim(rows_w, (1 - my_head) * half, half, 1), "head")

    def slab(w, s):
        return lax.dynamic_slice_in_dim(w, s * width, width, 0)

    weights = jnp.concatenate(
        [slab(keep_w, my_seq), slab(other_w, my_seq), slab(keep_w, 1 - my_seq), slab(other_w, 1 - my_seq)], 0
    )

    row_at = jnp.asarray(ROW_AT, jnp.int32)[me]
    place_of = jnp.asarray(PLACE_OF, jnp.int32)[me]
    early = scaled
    recv, assign, segs, scaled, weights, row_at, place_of = lax.optimization_barrier(
        (recv, assign, segs, scaled, weights, row_at, place_of)
    )

    attend = functools.partial(
        attend_rows, assign=assign, row_at=row_at, place_of=place_of, segs=segs, labels=advantage.shape[1], heads=mine
    )
    across, middle = ((0, 1), (1, 0), (2, 3), (3, 2)), ((1, 2), (2, 1))

    def send(x, perm, name):
        with jax.named_scope(name):
            return lax.ppermute(x, "dp", perm)

    inner = (me == 1) | (me == 2)

    from_2, mid_1 = send(early, across, "swap_0"), send(early, middle, "mid_0")

    far = attend((0,), recv)
    far_seq, far_head = swap(far, "seq", "far_seq"), swap(far, "head", "far_head")
    near = attend((1, 2, 3), recv)
    near, from_2 = lax.optimization_barrier((near, from_2))
    far_seq, near = lax.optimization_barrier((far_seq, near))
    far_diag = swap(far_seq, "head", "far_diag")
    near_seq, near_head = swap(near, "seq", "near_seq"), swap(near, "head", "near_head")
    (first,) = project((far, far_head, far_seq, far_diag), weights, row_len)
    near_diag = swap(near_seq, "head", "near_diag")
    second, third, own = project((near, near_head, near_seq, near_diag), weights, row_len)

    to_swap, from_2 = lax.optimization_barrier((jnp.where(inner, mid_1, first), from_2))
    swapped_1 = send(to_swap, across, "swap_1")
    mid_0 = send(from_2, middle, "mid_1")
    swapped_1, mid_0, second, third = lax.optimization_barrier((swapped_1, mid_0, second, third))
    swapped_2 = send(jnp.where(inner, mid_0, second), across, "swap_2")
    crossed_2 = send(add(first, swapped_1), middle, "mid_2")
    swapped_2, crossed_2 = lax.optimization_barrier((swapped_2, crossed_2))
    to_swap, second = lax.optimization_barrier((add(third, crossed_2), second))
    swapped_3 = send(to_swap, across, "swap_3")
    crossed_3 = send(add(second, swapped_2), middle, "mid_3")

    pieces = [jnp.where(inner, mid_0, swapped_2), jnp.where(inner, mid_1, swapped_1), from_2, scaled]
    others = [swap(x, "head", f"piece_{i}") for i, x in enumerate(pieces)]
    grad = weight_gradient((far, near), (far_seq, near_seq), pieces, others, my_seq, my_head)
    swapped_3, grad = lax.optimization_barrier((swapped_3, grad))
    mixed = own.astype(jnp.float32) + swapped_3.astype(jnp.float32) + crossed_3.astype(jnp.float32)
    return mixed.astype(jnp.bfloat16), grad.reshape(nseq * mine, 1, head_size, cols)


def solution(mesh):
    placed = (
        P(None, ("groups", "dp", "seq"), None, "head", None),
        P(("groups", "dp"), "seq", None),
        P(("groups", "dp"), None),
        P(("groups", "dp"), None),
        P("dp", "head", None, "seq"),
        P(("groups", "dp"), "seq"),
    )

    def body(projected, *rest):
        ndp, nseq = mesh.shape["dp"], mesh.shape["seq"]
        fits = projected.shape[2] % (ndp * nseq) == 0 and (ndp, nseq) == (4, 2)
        return (body_heads if fits else body_rows)(projected, *rest)

    return jax.shard_map(
        body,
        mesh=mesh,
        in_specs=placed,
        out_specs=(P(("groups", "dp"), ("seq", "head")), P(("groups", "dp"), "head", None, "seq")),
        check_vma=False,
    )
```
